32 devices in a mesh: gy: 4 (over z), gx: 8 (over y, x, core).
Axes of the slice: x: 2, y: 2, z: 4, core: 2. Of those that a mesh axis runs over, the one named last changes fastest.
Arguments:
- positions: float32 [3, 8, 32768], P(None, 'gx', 'gy'), may hold values from -6 to 6
- velocities: float32 [3, 8, 32768], P(None, 'gx', 'gy'), may hold values from -6 to 6
- radius: float32 [8, 32768], P('gx', 'gy'), may hold values from 0.6 to 1
- sphere_cell: int32 [8, 32768], P('gx', 'gy'), may hold values from -1 to 8191, as said below
- pair_route: int32 [8, 256, 1], P('gx', 'gy'), may hold values from 0 to 6; in each aligned block of 64 rows (0 to 63, 64 to 127, ..., all dimensions but the last counted through in order) at most 16 rows name the same one
- pair_mine: int32 [8, 256], P('gx', 'gy'), may hold values from 0 to 63
- pair_theirs: int32 [8, 256], P('gx', 'gy'), may hold values from 0 to 63
- brick_owner: int32 [8, 4], P('gx'), may hold values from 0 to 3, each once within a row
- fluid_velocity: float32 [3, 8, 8192], P(None, 'gx', 'gy'), may hold values from -6 to 6
- pressure_grad: float32 [3, 8, 8192], P(None, 'gx', 'gy'), may hold values from -6 to 6
Outputs:
- new_velocity: float32 [3, 8, 32768], P(None, 'gx', 'gy')
- drag_source: float32 [3, 8, 8192], P(None, 'gx', 'gy')
The draws below stay inside these ranges and needn't reach their ends.
Inputs may be any that keep to these rules, and one draw needn't show every extreme that they name: `pair_route`: the pairs of one device name one offset at most 16 times, a bound that some block reaches. `sphere_cell`: in every block of 128 slots the live slots come first and are half of the block or more; every device has a full block.
All inputs are finite; a program needn't handle non-finite values.
Results may differ from the reference program's by a relative error of at most 0.0003.
Values sent between devices are 32-bit elements; how exact they have to be, the bound alone decides.
A program may use at most 128 MiB of HBM per device.

```python
import math
import jax
import jax.numpy as jnp
import numpy as np
from jax import lax

BLOCK = 128
BLK_DEV = 64
CELLS_DEV = 2048
PAIRS_DEV = 64
CAP = 16
SPH_COL = 32768
PAIR_COL = 256
NCOL = 8192
N_GY = 4
N_GX = 8


def draw_sphere_cell(key, part):
    base = jax.random.fold_in(key, 11)
    first_key, second_key, third_key = jax.random.split(base, 3)
    live_count = jax.random.randint(first_key, (N_GX, N_GY, BLK_DEV), BLOCK // 2, BLOCK + 1)
    full_block = jax.random.randint(second_key, (N_GX, N_GY, 1), 0, BLK_DEV)
    live_count = jnp.where(jnp.arange(BLK_DEV)[None, None, :] == full_block, BLOCK, live_count)
    cells = jax.random.randint(third_key, (N_GX, N_GY, BLK_DEV, BLOCK), 0, NCOL)
    slots = jnp.arange(BLOCK)[None, None, None, :]
    result = jnp.where(slots < live_count[..., None], cells, -1)
    return result.reshape(N_GX, SPH_COL).astype(jnp.int32)


def set_ends(values, own_key, least, top_value):
    dims = values.shape
    spot = [jax.random.randint(jax.random.fold_in(own_key, axis), (), 0, dims[axis]) for axis in range(len(dims))]
    values = values.at[tuple(spot)].set(least)
    longest = dims.index(max(dims))
    spot[longest] = (spot[longest] + 1) % dims[longest]
    return values.at[tuple(spot)].set(top_value)


def steps_of(stream_key, extent, shards, low, largest):
    gain, own = 1.0, jax.random.fold_in(stream_key, 6)
    for axis_at, blocks in shards:
        heights = jnp.exp(jax.random.uniform(jax.random.fold_in(own, axis_at), (blocks,), jnp.float32, low / len(shards), largest / len(shards)))
        gain = gain * jnp.repeat(heights, extent[axis_at] // blocks).reshape([-1 if axis == axis_at else 1 for axis in range(len(extent))])
    return gain


def shared_out(stream_key, own, number, rows, amount, top, reach, skew):
    order = jax.random.permutation(stream_key, amount)
    heavy_load, ordinary = load_shares(amount, rows * top, reach, skew, True), load_shares(amount, rows * top, reach, skew, False)
    places = jnp.arange(amount)

    def named(sizes, offset_by):
        used = int((sizes > 0).sum())
        fixed = max(1, used // 4)
        moved = fixed + (places - fixed + offset_by * (used - fixed)) % max(1, amount - fixed)
        return jnp.zeros((amount,), jnp.int32).at[order[jnp.where(places < fixed, places, moved)]].set(jnp.asarray(sizes, jnp.int32))

    sizes = jnp.where(number % 4 == 0, named(heavy_load, number // 4), named(ordinary, number - number // 4 - 1))
    mixed = jax.random.permutation(jax.random.fold_in(own, 3), amount)
    giver, sink = mixed[0:amount // 2 * 2:2], mixed[1:amount // 2 * 2:2]
    margin = jnp.minimum(sizes[giver] - 1, reach - sizes[sink]) // 2
    margin = jnp.where((giver == order[0]) | (sink == order[0]) | (sizes[sink] == 0), 0, jnp.maximum(margin, 0))
    moved = jax.random.randint(jax.random.fold_in(own, 4), (amount // 2,), 0, 1 << 20) % (margin + 1)
    sizes = sizes.at[giver].add(-moved).at[sink].add(moved)
    labels = jnp.searchsorted(jnp.cumsum(sizes), jnp.arange(rows * top), side="right").astype(jnp.int32)
    grid = labels.reshape(top, rows).T
    grid = grid[jax.random.permutation(jax.random.fold_in(own, 1), rows)]
    offset_by = jax.random.randint(jax.random.fold_in(own, 2), (rows, 1), 0, top)
    return jnp.take_along_axis(grid, (jnp.arange(top)[None, :] + offset_by) % top, axis=1)


def load_shares(count, total, most, lean, full):
    portions = [(1 << 20) // math.isqrt(standing ** lean) + 1 for standing in range(1, count + 1)]
    largest = most if full else min(most, max(-(-total // count), total * portions[0] // sum(portions)))
    least = 1 if total - largest >= count - 1 else 0
    given, rest = [largest] + [least] * (count - 1), total - largest - least * (count - 1)
    while rest > 0:
        candidates = [i for i in range(1, count) if given[i] < largest] or [i for i in range(1, count) if given[i] < most]
        whole, remaining = sum([portions[i] for i in candidates]), rest
        for i in candidates:
            more = min(most - given[i], max(1, remaining * portions[i] // whole), rest)
            given[i] = given[i] + more
            rest = rest - more
    return np.array(given)


def noise(rng, shape, deviation, limit, cuts=(), kind=jnp.bfloat16):
    values = jax.random.normal(rng, shape, jnp.float32) * deviation
    if len(cuts) > 0:
        values = steps_of(rng, shape, cuts, -0.22, 0.18) * values
    return jnp.clip(values, min=-limit, max=limit).astype(kind)


def setup_inputs(seed: int = 0) -> dict:
    splits = jax.random.split(jax.random.key(seed), 11)
    positions = noise(splits[0], (3, N_GX, SPH_COL), 1.0, 6.0, ((1, 8), (2, 4)), jnp.float32)
    velocities = noise(splits[1], (3, N_GX, SPH_COL), 1.0, 6.0, ((1, 8), (2, 4)), jnp.float32)
    radius = jnp.clip(jnp.exp(math.log(1.0) - 0.5108256 * jax.random.uniform(splits[2], (N_GX, SPH_COL), jnp.float32) ** steps_of(splits[2], (N_GX, SPH_COL), ((0, 8), (1, 4)), -0.2, 0.2)), 0.6, 1.0)
    sphere_cell = draw_sphere_cell(jax.random.fold_in(splits[10], 71), 0)
    pair_route_keys = jax.random.split(jax.random.fold_in(splits[4], 1), N_GX * PAIR_COL // PAIRS_DEV)
    pair_route_turns = jax.random.permutation(jax.random.fold_in(splits[4], 3), N_GX * PAIR_COL // PAIRS_DEV)
    pair_route = jax.vmap(lambda own, number: shared_out(jax.random.fold_in(splits[4], 2), own, number, PAIRS_DEV, N_GX - 1, 1, CAP, 2))(pair_route_keys, pair_route_turns).reshape((N_GX, PAIR_COL, 1))
    pair_mine = set_ends(jax.random.randint(splits[5], (N_GX, PAIR_COL), 0, BLK_DEV), jax.random.fold_in(splits[5], 1), 0, BLK_DEV - 1).astype(jnp.int32)
    pair_theirs = set_ends(jax.random.randint(splits[6], (N_GX, PAIR_COL), 0, BLK_DEV), jax.random.fold_in(splits[6], 1), 0, BLK_DEV - 1).astype(jnp.int32)
    brick_owner = jax.vmap(lambda own: jax.random.permutation(own, N_GY))(jax.random.split(splits[7], N_GX)).reshape((N_GX, N_GY)).astype(jnp.int32)
    fluid_velocity = noise(splits[8], (3, N_GX, NCOL), 1.0, 6.0, ((1, 8), (2, 4)), jnp.float32)
    pressure_grad = noise(splits[9], (3, N_GX, NCOL), 1.0, 6.0, ((1, 8), (2, 4)), jnp.float32)
    return dict(positions=positions, velocities=velocities, radius=radius, sphere_cell=sphere_cell, pair_route=pair_route, pair_mine=pair_mine, pair_theirs=pair_theirs, brick_owner=brick_owner, fluid_velocity=fluid_velocity, pressure_grad=pressure_grad)


stiffness = 0.05
damping = 0.02
drag_coeff = 0.5
time_step = 0.2


def contact(left_state, right_state):
    offset = left_state[:, 0:3, :, None] - right_state[:, 0:3, None, :]
    dist_sq = offset[:, 0] * offset[:, 0] + offset[:, 1] * offset[:, 1] + offset[:, 2] * offset[:, 2]
    radius_sum = left_state[:, 6, :, None] + right_state[:, 6, None, :]
    weight = jnp.exp(-dist_sq / (2.0 * radius_sum * radius_sum)) * (left_state[:, 7, :, None] * right_state[:, 7, None, :])
    relative = left_state[:, 3:6, :, None] - right_state[:, 3:6, None, :]
    pulling = weight[:, None] * (stiffness * offset - damping * relative)
    return jnp.sum(pulling, axis=3), -jnp.sum(pulling, axis=2)


def contact_pair(pair_in):
    return contact(pair_in[0], pair_in[1])


def grouped(left_all, right_all):
    count_all = left_all.shape[0]
    group_size = math.gcd(count_all, 8)
    shaped = (left_all.reshape(count_all // group_size, group_size, 8, BLOCK),
              right_all.reshape(count_all // group_size, group_size, 8, BLOCK))
    on_left, on_right = lax.map(contact_pair, shaped)
    return on_left.reshape(count_all, 3, BLOCK), on_right.reshape(count_all, 3, BLOCK)


def reference(positions, velocities, radius, sphere_cell, pair_route, pair_mine, pair_theirs, brick_owner, fluid_velocity, pressure_grad):
    alive_mask = (sphere_cell >= 0).astype(jnp.float32)
    states = jnp.concatenate([positions, velocities, radius[None], alive_mask[None]], axis=0)
    states = states.reshape(8, N_GX, N_GY, BLK_DEV, BLOCK).transpose(1, 2, 3, 0, 4)

    def one_device(forces, flat_index):
        column = (flat_index // N_GY).astype(jnp.int32)
        row_index = (flat_index % N_GY).astype(jnp.int32)
        own_blocks = states[column, row_index]
        beside = jnp.concatenate([own_blocks[1:], jnp.zeros_like(own_blocks[:1])], axis=0)
        self_force, unused_self = grouped(own_blocks, own_blocks)
        near_force, back_force = grouped(own_blocks, beside)
        local_force = self_force + near_force + jnp.concatenate([jnp.zeros_like(back_force[:1]), back_force[:-1]], axis=0)
        start_at = (row_index * PAIRS_DEV).astype(jnp.int32)
        route_off = lax.dynamic_slice_in_dim(pair_route[column, :, 0], start_at, PAIRS_DEV)
        mine_index = lax.dynamic_slice_in_dim(pair_mine[column], start_at, PAIRS_DEV)
        theirs = lax.dynamic_slice_in_dim(pair_theirs[column], start_at, PAIRS_DEV)
        target = ((column + 1 + route_off) % N_GX).astype(jnp.int32)
        partner = states[target, row_index, theirs]
        on_owner, on_partner = grouped(own_blocks[mine_index], partner)
        forces = forces.at[column, row_index].add(local_force)
        forces = forces.at[column, row_index, mine_index].add(on_owner)
        forces = forces.at[target, row_index, theirs].add(on_partner)
        return forces, None

    start_forces = jnp.zeros((N_GX, N_GY, BLK_DEV, 3, BLOCK), jnp.float32)
    forces, unused_out = lax.scan(one_device, start_forces, jnp.arange(N_GX * N_GY, dtype=jnp.int32))
    contact_force = forces.transpose(3, 0, 1, 2, 4).reshape(3, N_GX, SPH_COL)

    block_of = jnp.clip(sphere_cell // CELLS_DEV, 0, N_GY - 1).astype(jnp.int32)
    within = sphere_cell % CELLS_DEV
    owner_of = jnp.take_along_axis(brick_owner, block_of, axis=1)
    storage = jnp.where(sphere_cell >= 0, owner_of * CELLS_DEV + within, 0).astype(jnp.int32)
    fluid_at = jnp.take_along_axis(fluid_velocity, storage[None], axis=2)
    grad_at = jnp.take_along_axis(pressure_grad, storage[None], axis=2)
    sphere_cube = radius * radius * radius
    drag_force = alive_mask * drag_coeff * radius * (fluid_at - velocities)
    fluid_force = drag_force - alive_mask * sphere_cube * grad_at
    new_velocity = velocities + time_step * (contact_force + fluid_force) / sphere_cube
    flat_cell = (jnp.arange(N_GX, dtype=jnp.int32)[:, None] * NCOL + storage).reshape(-1)
    deposit = jax.ops.segment_sum(-drag_force.reshape(3, -1).T, flat_cell, num_segments=N_GX * NCOL)
    drag_source = deposit.T.reshape(3, N_GX, NCOL)
    return new_velocity, drag_source
```

```python
import functools
import math

import jax
import jax.numpy as jnp
from jax import lax
from jax.experimental import pallas as pl
from jax.experimental.pallas import tpu as pltpu
from jax.sharding import PartitionSpec as P

stiffness = 0.05
damping = 0.02
drag_coeff = 0.5
time_step = 0.2
WIDTH = 128
NT = (((1,), (1,)), ((), ()))
NN = (((1,), (0,)), ((), ()))
VMEM = pl.BlockSpec(memory_space=pltpu.VMEM)
SMEM = pl.BlockSpec(memory_space=pltpu.SMEM)
LIMIT = 48 * 1024 * 1024


def split(value):
    high = value.astype(jnp.bfloat16)
    return high, (value - high.astype(jnp.float32)).astype(jnp.bfloat16)


def state_kernel(asked_ref, place_ref, speed_ref, radius_ref, cell_ref, state_ref, served_ref):
    alive = jnp.where(cell_ref[...] >= 0, 1.0, 0.0)
    for c in range(3):
        place = place_ref[c]
        state_ref[:, c, :] = (stiffness * place - damping * speed_ref[c]) * alive
        state_ref[:, 4 + c, :] = place
    state_ref[:, 3, :] = alive
    state_ref[:, 7, :] = radius_ref[...] * math.sqrt(2.0 * math.log(2.0))

    def serve(s, _):
        served_ref[s] = state_ref[jnp.clip(asked_ref[s], 0, state_ref.shape[0] - 1)]
        return 0

    lax.fori_loop(0, served_ref.shape[0], serve, 0, unroll=4)


def weights(columns, other):
    one = columns[:, 4:5] - other[4:5, :]
    two = columns[:, 5:6] - other[5:6, :]
    three = columns[:, 6:7] - other[6:7, :]
    reach = columns[:, 7:8] + other[7:8, :]
    dist_sq = one * one + two * two + three * three
    square = reach * reach
    guess = pl.reciprocal(square, approx=True)
    return split(jnp.exp2((dist_sq * guess) * (square * guess - 2.0)))


def stacked(state):
    return jnp.concatenate(split(state), axis=0)


def summed(lhs, pieces, dims):
    high, low = (
        lax.dot_general(lhs, piece, dims, preferred_element_type=jnp.float32) for piece in pieces
    )
    both = high + low
    return both[0:8] + both[8:16]


def contact_kernel(mine_ref, slot_ref, state_ref, partner_ref, acc_ref, back_ref, carry):
    blocks = state_ref.shape[0]
    pairs = mine_ref.shape[0]
    carry[...] = jnp.zeros_like(carry)

    def local(b, _):
        state = state_ref[b]
        after = jnp.minimum(b + 1, blocks - 1)
        beside = state_ref[after] * jnp.where(b + 1 < blocks, 1.0, 0.0)
        both = jnp.concatenate([state, beside], axis=1)
        pieces = weights(state.T, both)
        on_me = summed(stacked(both), pieces, NT)
        on_next = summed(stacked(state), [piece[:, WIDTH:] for piece in pieces], NN)
        acc_ref[b] = on_me + carry[...]
        carry[...] = on_next
        return 0

    lax.fori_loop(0, blocks, local, 0, unroll=4)

    def listed(p, _):
        mine = mine_ref[p]
        slot = slot_ref[p]
        state = state_ref[mine]
        other = partner_ref[slot]
        pieces = weights(state.T, other)
        on_me = summed(stacked(other), pieces, NT)
        on_other = summed(stacked(state), pieces, NN)
        acc_ref[mine] = acc_ref[mine] + on_me
        back_ref[slot] = on_other[0:4]
        return 0

    lax.fori_loop(0, pairs, listed, 0, unroll=4)


def fluid_kernel(tile, owner_ref, cell_ref, speed_ref, radius_ref, table_ref, fluid_ref, deposit_ref, table, total):
    ranks, fields, rows, _ = table_ref.shape
    high, low = split(table_ref[...].reshape(ranks * fields * rows, WIDTH))
    table[:, 0:WIDTH] = high
    table[:, WIDTH:] = low
    total[...] = jnp.zeros_like(total)

    def step(t, _):
        part = pl.ds(pl.multiple_of(t * tile, tile), tile)
        cell = cell_ref[:, part]
        alive = jnp.where(cell >= 0, 1.0, 0.0)
        safe = jnp.maximum(cell, 0)
        brick = safe // (rows * WIDTH)
        owner = jnp.zeros_like(cell)
        for k in range(ranks):
            owner = jnp.where(brick == k, owner_ref[0, k], owner)
        stored = jnp.where(cell >= 0, owner * (rows * WIDTH) + safe % (rows * WIDTH), 0)
        lane = lax.broadcasted_iota(jnp.int32, (WIDTH, tile), 0)
        hot = jnp.where(lane == stored % WIDTH, 1.0, 0.0).astype(jnp.bfloat16)
        row = lax.broadcasted_iota(jnp.int32, (ranks * rows, tile), 0)
        mask = (row == stored // WIDTH).reshape(ranks, 1, rows, tile)
        found = jnp.dot(
            table[...], jnp.concatenate([hot, hot], axis=0), preferred_element_type=jnp.float32
        ).reshape(ranks, fields, rows, tile)
        found = jnp.sum(jnp.where(mask, found, 0.0), axis=(0, 2))
        radii = radius_ref[:, part]
        scale = alive * drag_coeff * radii
        cube = alive * radii * radii * radii
        drags = []
        for c in range(3):
            drag = scale * (found[c : c + 1] - speed_ref[c, :, part])
            fluid_ref[c, :, part] = drag - cube * found[3 + c : 4 + c]
            drags.append(-drag)
        drags = jnp.concatenate(drags, axis=0).reshape(1, 3, 1, tile)
        spread = jnp.where(mask, drags, 0.0).reshape(ranks * 3 * rows, tile)
        high, low = split(spread)
        total[...] += lax.dot_general(
            high, hot, NT, preferred_element_type=jnp.float32
        ) + lax.dot_general(low, hot, NT, preferred_element_type=jnp.float32)
        return 0

    lax.fori_loop(0, cell_ref.shape[1] // tile, step, 0)
    deposit_ref[...] = total[...].reshape(ranks, 3, rows, WIDTH)


def final_kernel(asked_ref, acc_ref, back_ref, state_ref, fluid_ref, speed_ref, radius_ref, out_ref, force):
    force[...] = acc_ref[...]

    def add(s, _):
        block = asked_ref[s]

        @pl.when(block >= 0)
        def _():
            force[block, 0:4, :] = force[block, 0:4, :] + back_ref[s]

        return 0

    lax.fori_loop(0, asked_ref.shape[0], add, 0)
    radii = radius_ref[...]
    scale = time_step / (radii * radii * radii)
    alive = state_ref[:, 3, :]
    weight = force[:, 3, :]
    for c in range(3):
        contact = state_ref[:, c, :] * weight - alive * force[:, c, :]
        out_ref[c] = speed_ref[c] + scale * (contact + fluid_ref[c])


def on_device(
    positions,
    velocities,
    radius,
    sphere_cell,
    pair_route,
    pair_mine,
    pair_theirs,
    brick_owner,
    fluid_velocity,
    pressure_grad,
):
    f32 = jnp.float32
    sphere_total = positions.shape[2]
    blocks = sphere_total // WIDTH
    gy_count = lax.axis_size("gy")
    gx_count = lax.axis_size("gx")
    cells_dev = fluid_velocity.shape[2]
    rows = cells_dev // WIDTH
    pair_total = pair_route.shape[1]
    capacity = max(2, 2 * pair_total // gx_count)
    slot_total = gx_count * capacity
    params = pltpu.CompilerParams(vmem_limit_bytes=LIMIT)

    target = (lax.axis_index("gx") + 1 + pair_route[0, :, 0]) % gx_count
    pair_ids = jnp.arange(pair_total, dtype=jnp.int32)
    earlier = (target[:, None] == target[None, :]) & (pair_ids[None, :] < pair_ids[:, None])
    slot = target * capacity + jnp.sum(earlier.astype(jnp.int32), axis=1)
    match = slot[None, :] == jnp.arange(slot_total, dtype=jnp.int32)[:, None]
    wanted = jnp.sum(jnp.where(match, pair_theirs[0][None, :] + 1, 0), axis=1) - 1
    asked = lax.all_to_all(
        wanted.reshape(gx_count, capacity), "gx", split_axis=0, concat_axis=0, tiled=True
    ).reshape(-1)

    fields = jnp.concatenate([fluid_velocity[:, 0], pressure_grad[:, 0]], axis=0)
    fields = fields.reshape(1, 6, rows, WIDTH)
    table = lax.all_to_all(
        jnp.broadcast_to(fields, (gy_count, 6, rows, WIDTH)),
        "gy",
        split_axis=0,
        concat_axis=0,
        tiled=True,
    )

    states, served = pl.pallas_call(
        state_kernel,
        out_shape=(
            jax.ShapeDtypeStruct((blocks, 8, WIDTH), f32),
            jax.ShapeDtypeStruct((slot_total, 8, WIDTH), f32),
        ),
        in_specs=[SMEM] + [VMEM] * 4,
        out_specs=(VMEM, VMEM),
        compiler_params=params,
        name="states",
    )(
        asked,
        positions.reshape(3, blocks, WIDTH),
        velocities.reshape(3, blocks, WIDTH),
        radius.reshape(blocks, WIDTH),
        sphere_cell.reshape(blocks, WIDTH),
    )
    partner = lax.all_to_all(
        served.reshape(gx_count, capacity, 8, WIDTH), "gx", split_axis=0, concat_axis=0, tiled=True
    ).reshape(slot_total, 8, WIDTH)

    tile = math.gcd(sphere_total, 512)
    fluid, deposit = pl.pallas_call(
        functools.partial(fluid_kernel, tile),
        out_shape=(
            jax.ShapeDtypeStruct((3, 1, sphere_total), f32),
            jax.ShapeDtypeStruct((gy_count, 3, rows, WIDTH), f32),
        ),
        in_specs=[SMEM] + [VMEM] * 4,
        out_specs=(VMEM, VMEM),
        scratch_shapes=[
            pltpu.VMEM((gy_count * 6 * rows, 2 * WIDTH), jnp.bfloat16),
            pltpu.VMEM((gy_count * 3 * rows, WIDTH), f32),
        ],
        compiler_params=params,
        cost_estimate=pl.CostEstimate(flops=4000000000, bytes_accessed=1000000, transcendentals=0),
        name="fluid",
    )(brick_owner, sphere_cell, velocities, radius, table)
    deposits = lax.all_to_all(deposit, "gy", split_axis=0, concat_axis=0, tiled=True)
    drag_source = jnp.sum(deposits, axis=0).reshape(3, 1, cells_dev)

    acc, back = pl.pallas_call(
        contact_kernel,
        out_shape=(
            jax.ShapeDtypeStruct((blocks, 8, WIDTH), f32),
            jax.ShapeDtypeStruct((slot_total, 4, WIDTH), f32),
        ),
        in_specs=[SMEM, SMEM, VMEM, VMEM],
        out_specs=(VMEM, VMEM),
        scratch_shapes=[pltpu.VMEM((8, WIDTH), f32)],
        compiler_params=params,
        cost_estimate=pl.CostEstimate(
            flops=8000000000, bytes_accessed=1500000, transcendentals=6000000
        ),
        name="contact",
    )(pair_mine[0], slot, states, partner)
    returned = lax.all_to_all(
        back.reshape(gx_count, capacity, 4, WIDTH), "gx", split_axis=0, concat_axis=0, tiled=True
    ).reshape(slot_total, 4, WIDTH)
    speed = velocities.reshape(3, blocks, WIDTH)
    new_velocity = pl.pallas_call(
        final_kernel,
        out_shape=jax.ShapeDtypeStruct((3, blocks, WIDTH), f32),
        in_specs=[SMEM] + [VMEM] * 6,
        out_specs=VMEM,
        scratch_shapes=[pltpu.VMEM((blocks, 8, WIDTH), f32)],
        compiler_params=params,
        name="final",
    )(asked, acc, returned, states, fluid.reshape(3, blocks, WIDTH), speed, radius.reshape(blocks, WIDTH))
    return (new_velocity.reshape(3, 1, sphere_total), drag_source)


def solution(mesh):
    placed = (
        P(None, "gx", "gy"),
        P(None, "gx", "gy"),
        P("gx", "gy"),
        P("gx", "gy"),
        P("gx", "gy", None),
        P("gx", "gy"),
        P("gx", "gy"),
        P("gx", None),
        P(None, "gx", "gy"),
        P(None, "gx", "gy"),
    )
    return jax.shard_map(
        on_device,
        mesh=mesh,
        in_specs=placed,
        out_specs=(P(None, "gx", "gy"), P(None, "gx", "gy")),
        check_vma=False,
    )
```

```python
import functools
import math

import jax
import jax.numpy as jnp
from jax import lax
from jax.experimental import pallas as pl
from jax.experimental.pallas import tpu as pltpu
from jax.sharding import PartitionSpec as P

stiffness = 0.05
damping = 0.02
drag_coeff = 0.5
time_step = 0.2
WIDTH = 128
NT = (((1,), (1,)), ((), ()))
NN = (((1,), (0,)), ((), ()))
VMEM = pl.BlockSpec(memory_space=pltpu.VMEM)
SMEM = pl.BlockSpec(memory_space=pltpu.SMEM)
LIMIT = 48 * 1024 * 1024


def split(value):
    high = value.astype(jnp.bfloat16)
    return high, (value - high.astype(jnp.float32)).astype(jnp.bfloat16)


def greet(counts):
    barrier = pltpu.get_barrier_semaphore()
    total = 0
    for axis, count in counts.items():
        me = lax.axis_index(axis)
        for step in range(1, count):
            pl.semaphore_signal(
                barrier,
                inc=1,
                device_id={axis: lax.rem(me + step, count)},
                device_id_type=pl.DeviceIdType.MESH,
            )
        total += count - 1
    pl.semaphore_wait(barrier, total)


def start_copies(axis, count, source, landing, send_sem, recv_sem, same=False):
    me = lax.axis_index(axis)
    copies = []
    for step in range(1, count):
        peer = lax.rem(me + step, count)
        copy = pltpu.make_async_remote_copy(
            src_ref=source if same else source.at[peer],
            dst_ref=landing.at[me],
            send_sem=send_sem.at[step],
            recv_sem=recv_sem.at[step],
            device_id={axis: peer},
            device_id_type=pl.DeviceIdType.MESH,
        )
        copy.start()
        copies.append(copy)
    return copies


def exchange_kernel(counts, gx_ref, gy_ref, gx_out, gy_out, xs, xr, ys, yr):
    greet(counts)
    copies = start_copies("gx", counts["gx"], gx_ref, gx_out, xs, xr)
    copies += start_copies("gy", counts["gy"], gy_ref, gy_out, ys, yr, True)
    me = lax.axis_index("gx")
    gx_out[me] = gx_ref[me]
    me = lax.axis_index("gy")
    gy_out[me] = gy_ref[...]
    for copy in copies:
        copy.wait()


def exchange(counts, gx_value, gy_value):
    return pl.pallas_call(
        functools.partial(exchange_kernel, counts),
        out_shape=(
            jax.ShapeDtypeStruct(gx_value.shape, gx_value.dtype),
            jax.ShapeDtypeStruct((counts["gy"],) + gy_value.shape, gy_value.dtype),
        ),
        in_specs=[VMEM, VMEM],
        out_specs=(VMEM, VMEM),
        scratch_shapes=[
            pltpu.SemaphoreType.DMA((counts[axis],)) for axis in ("gx", "gx", "gy", "gy")
        ],
        compiler_params=pltpu.CompilerParams(
            vmem_limit_bytes=LIMIT, collective_id=0, has_side_effects=True
        ),
        name="exchange",
    )(gx_value, gy_value)


def state_kernel(asked_ref, place_ref, speed_ref, radius_ref, cell_ref, state_ref, served_ref):
    alive = jnp.where(cell_ref[...] >= 0, 1.0, 0.0)
    for c in range(3):
        place = place_ref[c]
        state_ref[:, c, :] = (stiffness * place - damping * speed_ref[c]) * alive
        state_ref[:, 4 + c, :] = place
    state_ref[:, 3, :] = alive
    state_ref[:, 7, :] = radius_ref[...] * math.sqrt(2.0 * math.log(2.0))

    def serve(s, _):
        served_ref[s] = state_ref[jnp.clip(asked_ref[s], 0, state_ref.shape[0] - 1)]
        return 0

    lax.fori_loop(0, served_ref.shape[0], serve, 0, unroll=4)


def weights(columns, other):
    one = columns[:, 4:5] - other[4:5, :]
    two = columns[:, 5:6] - other[5:6, :]
    three = columns[:, 6:7] - other[6:7, :]
    reach = columns[:, 7:8] + other[7:8, :]
    dist_sq = one * one + two * two + three * three
    square = reach * reach
    guess = pl.reciprocal(square, approx=True)
    return split(jnp.exp2((dist_sq * guess) * (square * guess - 2.0)))


def stacked(state):
    return jnp.concatenate(split(state), axis=0)


def summed(lhs, pieces, dims):
    high, low = (
        lax.dot_general(lhs, piece, dims, preferred_element_type=jnp.float32) for piece in pieces
    )
    both = high + low
    return both[0:8] + both[8:16]


def listed_kernel(mine_ref, slot_ref, state_ref, partner_ref, acc_ref, back_ref):
    acc_ref[...] = jnp.zeros_like(acc_ref)

    def listed(p, _):
        mine = mine_ref[p]
        slot = slot_ref[p]
        state = state_ref[mine]
        other = partner_ref[slot]
        pieces = weights(state.T, other)
        on_me = summed(stacked(other), pieces, NT)
        on_other = summed(stacked(state), pieces, NN)
        acc_ref[mine] = acc_ref[mine] + on_me
        back_ref[pl.ds(pl.multiple_of(slot * 4, 4), 4), :] = on_other[0:4]
        return 0

    lax.fori_loop(0, mine_ref.shape[0], listed, 0, unroll=4)


def local_kernel(
    counts, state_ref, listed_ref, gx_ref, gy_ref, acc_ref, gx_out, gy_out, carry, xs, xr, ys, yr
):
    greet(counts)
    copies = start_copies("gx", counts["gx"], gx_ref, gx_out, xs, xr)
    copies += start_copies("gy", counts["gy"], gy_ref, gy_out, ys, yr)
    me = lax.axis_index("gx")
    gx_out[me] = gx_ref[me]
    me = lax.axis_index("gy")
    gy_out[me] = gy_ref[me]
    blocks = state_ref.shape[0]
    carry[...] = jnp.zeros_like(carry)

    def local(b, _):
        state = state_ref[b]
        after = lax.rem(b + 1, blocks)
        beside = state_ref[after] * jnp.where(after > 0, 1.0, 0.0)
        both = jnp.concatenate([state, beside], axis=1)
        pieces = weights(state.T, both)
        on_me = summed(stacked(both), pieces, NT)
        on_next = summed(stacked(state), [piece[:, WIDTH:] for piece in pieces], NN)
        acc_ref[b] = listed_ref[b] + on_me + carry[...]
        carry[...] = on_next
        return 0

    lax.fori_loop(0, blocks, local, 0, unroll=4)
    for copy in copies:
        copy.wait()


def fluid_kernel(
    tile,
    gx_count,
    owner_ref,
    cell_ref,
    speed_ref,
    radius_ref,
    table_ref,
    served_ref,
    fluid_ref,
    deposit_ref,
    partner_ref,
    table,
    total,
    send_sem,
    recv_sem,
):
    greet({"gx": gx_count})
    copies = start_copies("gx", gx_count, served_ref, partner_ref, send_sem, recv_sem)
    me = lax.axis_index("gx")
    partner_ref[me] = served_ref[me]
    ranks, fields, rows, _ = table_ref.shape
    high, low = split(table_ref[...].reshape(ranks * fields * rows, WIDTH))
    table[:, 0:WIDTH] = high
    table[:, WIDTH:] = low
    total[...] = jnp.zeros_like(total)

    def step(t, _):
        part = pl.ds(pl.multiple_of(t * tile, tile), tile)
        cell = cell_ref[:, part]
        alive = jnp.where(cell >= 0, 1.0, 0.0)
        safe = jnp.maximum(cell, 0)
        brick = safe // (rows * WIDTH)
        owner = jnp.zeros_like(cell)
        for k in range(ranks):
            owner = jnp.where(brick == k, owner_ref[0, k], owner)
        stored = jnp.where(cell >= 0, owner * (rows * WIDTH) + safe % (rows * WIDTH), 0)
        lane = lax.broadcasted_iota(jnp.int32, (WIDTH, tile), 0)
        hot = jnp.where(lane == stored % WIDTH, 1.0, 0.0).astype(jnp.bfloat16)
        row = lax.broadcasted_iota(jnp.int32, (ranks * rows, tile), 0)
        mask = (row == stored // WIDTH).reshape(ranks, 1, rows, tile)
        found = jnp.dot(
            table[...], jnp.concatenate([hot, hot], axis=0), preferred_element_type=jnp.float32
        ).reshape(ranks, fields, rows, tile)
        found = jnp.sum(jnp.where(mask, found, 0.0), axis=(0, 2))
        radii = radius_ref[:, part]
        scale = alive * drag_coeff * radii
        cube = alive * radii * radii * radii
        drags = []
        for c in range(3):
            drag = scale * (found[c : c + 1] - speed_ref[c, :, part])
            fluid_ref[c, :, part] = drag - cube * found[3 + c : 4 + c]
            drags.append(-drag)
        drags = jnp.concatenate(drags, axis=0).reshape(1, 3, 1, tile)
        spread = jnp.where(mask, drags, 0.0).reshape(ranks * 3 * rows, tile)
        high, low = split(spread)
        total[...] += lax.dot_general(
            high, hot, NT, preferred_element_type=jnp.float32
        ) + lax.dot_general(low, hot, NT, preferred_element_type=jnp.float32)
        return 0

    lax.fori_loop(0, cell_ref.shape[1] // tile, step, 0)
    deposit_ref[...] = total[...].reshape(ranks, 3, rows, WIDTH)
    for copy in copies:
        copy.wait()


def final_kernel(
    asked_ref,
    acc_ref,
    back_ref,
    state_ref,
    fluid_ref,
    speed_ref,
    radius_ref,
    deposits_ref,
    out_ref,
    source_ref,
    force,
):
    source_ref[...] = jnp.sum(deposits_ref[...], axis=0)
    force[...] = acc_ref[...]

    def add(s, _):
        block = asked_ref[s]

        @pl.when(block >= 0)
        def _():
            force[block, 0:4, :] = force[block, 0:4, :] + back_ref[pl.ds(pl.multiple_of(s * 4, 4), 4), :]

        return 0

    lax.fori_loop(0, asked_ref.shape[0], add, 0)
    radii = radius_ref[...]
    scale = time_step / (radii * radii * radii)
    alive = state_ref[:, 3, :]
    weight = force[:, 3, :]
    for c in range(3):
        contact = state_ref[:, c, :] * weight - alive * force[:, c, :]
        out_ref[c] = speed_ref[c] + scale * (contact + fluid_ref[c])


def on_device(
    positions,
    velocities,
    radius,
    sphere_cell,
    pair_route,
    pair_mine,
    pair_theirs,
    brick_owner,
    fluid_velocity,
    pressure_grad,
):
    f32 = jnp.float32
    sphere_total = positions.shape[2]
    blocks = sphere_total // WIDTH
    gy_count = lax.axis_size("gy")
    gx_count = lax.axis_size("gx")
    cells_dev = fluid_velocity.shape[2]
    rows = cells_dev // WIDTH
    pair_total = pair_route.shape[1]
    capacity = max(2, 2 * pair_total // gx_count)
    slot_total = gx_count * capacity
    params = pltpu.CompilerParams(vmem_limit_bytes=LIMIT)

    counts = {"gx": gx_count, "gy": gy_count}

    target = (lax.axis_index("gx") + 1 + pair_route[0, :, 0]) % gx_count
    pair_ids = jnp.arange(pair_total, dtype=jnp.int32)
    earlier = (target[:, None] == target[None, :]) & (pair_ids[None, :] < pair_ids[:, None])
    slot = target * capacity + jnp.sum(earlier.astype(jnp.int32), axis=1)
    match = slot[None, :] == jnp.arange(slot_total, dtype=jnp.int32)[:, None]
    wanted = jnp.sum(jnp.where(match, pair_theirs[0][None, :] + 1, 0), axis=1) - 1
    wanted = jnp.pad(
        wanted.reshape(gx_count, 1, capacity),
        ((0, 0), (0, 0), (0, WIDTH - capacity)),
        constant_values=-1,
    )
    fields = jnp.concatenate([fluid_velocity[:, 0], pressure_grad[:, 0]], axis=0)
    asked, table = exchange(counts, wanted, fields.reshape(6, rows, WIDTH))
    asked = asked[:, 0, :capacity].reshape(-1)

    states, served = pl.pallas_call(
        state_kernel,
        out_shape=(
            jax.ShapeDtypeStruct((blocks, 8, WIDTH), f32),
            jax.ShapeDtypeStruct((slot_total, 8, WIDTH), f32),
        ),
        in_specs=[SMEM] + [VMEM] * 4,
        out_specs=(VMEM, VMEM),
        compiler_params=params,
        name="states",
    )(
        asked,
        positions.reshape(3, blocks, WIDTH),
        velocities.reshape(3, blocks, WIDTH),
        radius.reshape(blocks, WIDTH),
        sphere_cell.reshape(blocks, WIDTH),
    )
    tile = math.gcd(sphere_total, 512)
    fluid, deposit, partner = pl.pallas_call(
        functools.partial(fluid_kernel, tile, gx_count),
        out_shape=(
            jax.ShapeDtypeStruct((3, 1, sphere_total), f32),
            jax.ShapeDtypeStruct((gy_count, 3, rows, WIDTH), f32),
            jax.ShapeDtypeStruct((gx_count, capacity * 8, WIDTH), f32),
        ),
        in_specs=[SMEM] + [VMEM] * 5,
        out_specs=(VMEM, VMEM, VMEM),
        scratch_shapes=[
            pltpu.VMEM((gy_count * 6 * rows, 2 * WIDTH), jnp.bfloat16),
            pltpu.VMEM((gy_count * 3 * rows, WIDTH), f32),
            pltpu.SemaphoreType.DMA((gx_count,)),
            pltpu.SemaphoreType.DMA((gx_count,)),
        ],
        compiler_params=pltpu.CompilerParams(
            vmem_limit_bytes=LIMIT, collective_id=1, has_side_effects=True
        ),
        cost_estimate=pl.CostEstimate(flops=4000000000, bytes_accessed=1000000, transcendentals=0),
        name="fluid",
    )(
        brick_owner,
        sphere_cell,
        velocities,
        radius,
        table,
        served.reshape(gx_count, capacity * 8, WIDTH),
    )
    partner = partner.reshape(slot_total, 8, WIDTH)
    listed, back = pl.pallas_call(
        listed_kernel,
        out_shape=(
            jax.ShapeDtypeStruct((blocks, 8, WIDTH), f32),
            jax.ShapeDtypeStruct((slot_total * 4, WIDTH), f32),
        ),
        in_specs=[SMEM, SMEM, VMEM, VMEM],
        out_specs=(VMEM, VMEM),
        compiler_params=params,
        name="listed",
    )(pair_mine[0], slot, states, partner)
    acc, returned, deposits = pl.pallas_call(
        functools.partial(local_kernel, counts),
        out_shape=(
            jax.ShapeDtypeStruct((blocks, 8, WIDTH), f32),
            jax.ShapeDtypeStruct((gx_count, capacity * 4, WIDTH), f32),
            jax.ShapeDtypeStruct(deposit.shape, f32),
        ),
        in_specs=[VMEM] * 4,
        out_specs=(VMEM, VMEM, VMEM),
        scratch_shapes=[pltpu.VMEM((8, WIDTH), f32)]
        + [pltpu.SemaphoreType.DMA((counts[axis],)) for axis in ("gx", "gx", "gy", "gy")],
        compiler_params=pltpu.CompilerParams(
            vmem_limit_bytes=LIMIT, collective_id=2, has_side_effects=True
        ),
        name="local",
    )(states, listed, back.reshape(gx_count, capacity * 4, WIDTH), deposit)
    returned = returned.reshape(slot_total * 4, WIDTH)
    speed = velocities.reshape(3, blocks, WIDTH)
    new_velocity, drag_source = pl.pallas_call(
        final_kernel,
        out_shape=(
            jax.ShapeDtypeStruct((3, blocks, WIDTH), f32),
            jax.ShapeDtypeStruct((3, rows, WIDTH), f32),
        ),
        in_specs=[SMEM] + [VMEM] * 7,
        out_specs=(VMEM, VMEM),
        scratch_shapes=[pltpu.VMEM((blocks, 8, WIDTH), f32)],
        compiler_params=params,
        name="final",
    )(
        asked,
        acc,
        returned,
        states,
        fluid.reshape(3, blocks, WIDTH),
        speed,
        radius.reshape(blocks, WIDTH),
        deposits,
    )
    return (new_velocity.reshape(3, 1, sphere_total), drag_source.reshape(3, 1, cells_dev))


def solution(mesh):
    placed = (
        P(None, "gx", "gy"),
        P(None, "gx", "gy"),
        P("gx", "gy"),
        P("gx", "gy"),
        P("gx", "gy", None),
        P("gx", "gy"),
        P("gx", "gy"),
        P("gx", None),
        P(None, "gx", "gy"),
        P(None, "gx", "gy"),
    )
    return jax.shard_map(
        on_device,
        mesh=mesh,
        in_specs=placed,
        out_specs=(P(None, "gx", "gy"), P(None, "gx", "gy")),
        check_vma=False,
    )
```

```python
import functools
import math

import jax
import jax.numpy as jnp
from jax import lax
from jax.experimental import pallas as pl
from jax.experimental.pallas import tpu as pltpu
from jax.sharding import PartitionSpec as P

stiffness = 0.05
damping = 0.02
drag_coeff = 0.5
time_step = 0.2
WIDTH = 128
NT = (((1,), (1,)), ((), ()))
NN = (((1,), (0,)), ((), ()))
VMEM = pl.BlockSpec(memory_space=pltpu.VMEM)
SMEM = pl.BlockSpec(memory_space=pltpu.SMEM)
LIMIT = 48 * 1024 * 1024


def split(value):
    high = value.astype(jnp.bfloat16)
    return high, (value - high.astype(jnp.float32)).astype(jnp.bfloat16)


def greet(counts):
    barrier = pltpu.get_barrier_semaphore()
    total = 0
    for axis, count in counts.items():
        me = lax.axis_index(axis)
        for step in range(1, count):
            pl.semaphore_signal(
                barrier,
                inc=1,
                device_id={axis: lax.rem(me + step, count)},
                device_id_type=pl.DeviceIdType.MESH,
            )
        total += count - 1
    pl.semaphore_wait(barrier, total)


def start_copies(axis, count, source, landing, send_sem, recv_sem, same=False):
    me = lax.axis_index(axis)
    copies = []
    for step in range(1, count):
        peer = lax.rem(me + step, count)
        copy = pltpu.make_async_remote_copy(
            src_ref=source if same else source.at[peer],
            dst_ref=landing.at[me],
            send_sem=send_sem.at[step],
            recv_sem=recv_sem.at[step],
            device_id={axis: peer},
            device_id_type=pl.DeviceIdType.MESH,
        )
        copy.start()
        copies.append(copy)
    return copies


def exchange_kernel(counts, gx_ref, gy_ref, gx_out, gy_out, xs, xr, ys, yr):
    greet(counts)
    copies = start_copies("gx", counts["gx"], gx_ref, gx_out, xs, xr)
    copies += start_copies("gy", counts["gy"], gy_ref, gy_out, ys, yr, True)
    me = lax.axis_index("gx")
    gx_out[me] = gx_ref[me]
    me = lax.axis_index("gy")
    gy_out[me] = gy_ref[...]
    for copy in copies:
        copy.wait()


def exchange(counts, gx_value, gy_value):
    return pl.pallas_call(
        functools.partial(exchange_kernel, counts),
        out_shape=(
            jax.ShapeDtypeStruct(gx_value.shape, gx_value.dtype),
            jax.ShapeDtypeStruct((counts["gy"],) + gy_value.shape, gy_value.dtype),
        ),
        in_specs=[VMEM, VMEM],
        out_specs=(VMEM, VMEM),
        scratch_shapes=[
            pltpu.SemaphoreType.DMA((counts[axis],)) for axis in ("gx", "gx", "gy", "gy")
        ],
        compiler_params=pltpu.CompilerParams(
            vmem_limit_bytes=LIMIT, collective_id=0, has_side_effects=True
        ),
        name="exchange",
    )(gx_value, gy_value)


def state_kernel(asked_ref, place_ref, speed_ref, radius_ref, cell_ref, state_ref, served_ref):
    alive = jnp.where(cell_ref[...] >= 0, 1.0, 0.0)
    for c in range(3):
        place = place_ref[c]
        state_ref[:, c, :] = (stiffness * place - damping * speed_ref[c]) * alive
        state_ref[:, 4 + c, :] = place
    state_ref[:, 3, :] = alive
    state_ref[:, 7, :] = radius_ref[...] * math.sqrt(2.0 * math.log(2.0))

    def serve(s, _):
        served_ref[s] = state_ref[jnp.clip(asked_ref[s], 0, state_ref.shape[0] - 1)]
        return 0

    lax.fori_loop(0, served_ref.shape[0], serve, 0, unroll=4)


def weights(columns, other):
    one = columns[:, 4:5] - other[4:5, :]
    two = columns[:, 5:6] - other[5:6, :]
    three = columns[:, 6:7] - other[6:7, :]
    reach = columns[:, 7:8] + other[7:8, :]
    dist_sq = one * one + two * two + three * three
    square = reach * reach
    guess = pl.reciprocal(square, approx=True)
    return split(jnp.exp2((dist_sq * guess) * (square * guess - 2.0)))


def stacked(state):
    return jnp.concatenate(split(state), axis=0)


def summed(lhs, pieces, dims):
    high, low = (
        lax.dot_general(lhs, piece, dims, preferred_element_type=jnp.float32) for piece in pieces
    )
    both = high + low
    return both[0:8] + both[8:16]


def listed_kernel(mine_ref, slot_ref, state_ref, partner_ref, acc_ref, back_ref):
    acc_ref[...] = jnp.zeros_like(acc_ref)

    pairs = mine_ref.shape[0]
    batch = math.gcd(pairs, 8)

    def listed(step, _):
        found = []
        states = [state_ref[mine_ref[step * batch + k]] for k in range(batch)]
        columns = jnp.concatenate(states, axis=0).T
        for k in range(batch):
            mine = mine_ref[step * batch + k]
            slot = slot_ref[step * batch + k]
            state = states[k]
            other = partner_ref[slot]
            pieces = weights(columns[:, 8 * k : 8 * k + 8], other)
            on_me = summed(stacked(other), pieces, NT)
            on_other = summed(stacked(state), pieces, NN)
            found.append((mine, slot, on_me, on_other))
        for mine, slot, on_me, on_other in found:
            acc_ref[mine] = acc_ref[mine] + on_me
            back_ref[pl.ds(pl.multiple_of(slot * 4, 4), 4), :] = on_other[0:4]
        return 0

    lax.fori_loop(0, pairs // batch, listed, 0)


def local_kernel(
    counts, state_ref, listed_ref, gx_ref, gy_ref, acc_ref, gx_out, gy_out, carry, xs, xr, ys, yr
):
    greet(counts)
    copies = start_copies("gx", counts["gx"], gx_ref, gx_out, xs, xr)
    copies += start_copies("gy", counts["gy"], gy_ref, gy_out, ys, yr)
    me = lax.axis_index("gx")
    gx_out[me] = gx_ref[me]
    me = lax.axis_index("gy")
    gy_out[me] = gy_ref[me]
    blocks = state_ref.shape[0]
    carry[...] = jnp.zeros_like(carry)

    batch = math.gcd(blocks, 8)

    def local(step, _):
        first = step * batch
        states = [state_ref[first + k] for k in range(batch)]
        after = lax.rem(first + batch, blocks)
        columns = jnp.concatenate(states, axis=0).T
        states.append(state_ref[after] * jnp.where(after > 0, 1.0, 0.0))
        found = []
        for k in range(batch):
            both = jnp.concatenate(states[k : k + 2], axis=1)
            pieces = weights(columns[:, 8 * k : 8 * k + 8], both)
            on_me = summed(stacked(both), pieces, NT)
            on_next = summed(stacked(states[k]), [piece[:, WIDTH:] for piece in pieces], NN)
            found.append((on_me, on_next))
        before = carry[...]
        for k in range(batch):
            acc_ref[first + k] = listed_ref[first + k] + found[k][0] + before
            before = found[k][1]
        carry[...] = before
        return 0

    lax.fori_loop(0, blocks // batch, local, 0)
    for copy in copies:
        copy.wait()


def fluid_kernel(
    tile,
    gx_count,
    owner_ref,
    cell_ref,
    speed_ref,
    radius_ref,
    table_ref,
    served_ref,
    fluid_ref,
    deposit_ref,
    partner_ref,
    table,
    total,
    send_sem,
    recv_sem,
):
    greet({"gx": gx_count})
    copies = start_copies("gx", gx_count, served_ref, partner_ref, send_sem, recv_sem)
    me = lax.axis_index("gx")
    partner_ref[me] = served_ref[me]
    ranks, fields, rows, _ = table_ref.shape
    high, low = split(table_ref[...].reshape(ranks * fields * rows, WIDTH))
    table[:, 0:WIDTH] = high
    table[:, WIDTH:] = low
    total[...] = jnp.zeros_like(total)

    def step(t, _):
        part = pl.ds(pl.multiple_of(t * tile, tile), tile)
        cell = cell_ref[:, part]
        alive = jnp.where(cell >= 0, 1.0, 0.0)
        safe = jnp.maximum(cell, 0)
        brick = safe // (rows * WIDTH)
        owner = jnp.zeros_like(cell)
        for k in range(ranks):
            owner = jnp.where(brick == k, owner_ref[0, k], owner)
        stored = jnp.where(cell >= 0, owner * (rows * WIDTH) + safe % (rows * WIDTH), 0)
        lane = lax.broadcasted_iota(jnp.int32, (WIDTH, tile), 0)
        hot = jnp.where(lane == stored % WIDTH, 1.0, 0.0).astype(jnp.bfloat16)
        row = lax.broadcasted_iota(jnp.int32, (ranks * rows, tile), 0)
        mask = (row == stored // WIDTH).reshape(ranks, 1, rows, tile)
        found = jnp.dot(
            table[...], jnp.concatenate([hot, hot], axis=0), preferred_element_type=jnp.float32
        ).reshape(ranks, fields, rows, tile)
        found = jnp.sum(jnp.where(mask, found, 0.0), axis=(0, 2))
        radii = radius_ref[:, part]
        scale = alive * drag_coeff * radii
        cube = alive * radii * radii * radii
        drags = []
        for c in range(3):
            drag = scale * (found[c : c + 1] - speed_ref[c, :, part])
            fluid_ref[c, :, part] = drag - cube * found[3 + c : 4 + c]
            drags.append(-drag)
        drags = jnp.concatenate(drags, axis=0).reshape(1, 3, 1, tile)
        spread = jnp.where(mask, drags, 0.0).reshape(ranks * 3 * rows, tile)
        high, low = split(spread)
        total[...] += lax.dot_general(
            high, hot, NT, preferred_element_type=jnp.float32
        ) + lax.dot_general(low, hot, NT, preferred_element_type=jnp.float32)
        return 0

    lax.fori_loop(0, cell_ref.shape[1] // tile, step, 0)
    deposit_ref[...] = total[...].reshape(ranks, 3, rows, WIDTH)
    for copy in copies:
        copy.wait()


def final_kernel(
    asked_ref,
    acc_ref,
    back_ref,
    state_ref,
    fluid_ref,
    speed_ref,
    radius_ref,
    deposits_ref,
    out_ref,
    source_ref,
    force,
):
    source_ref[...] = jnp.sum(deposits_ref[...], axis=0)
    force[...] = acc_ref[...]

    def add(s, _):
        block = asked_ref[s]

        @pl.when(block >= 0)
        def _():
            force[block, 0:4, :] = force[block, 0:4, :] + back_ref[pl.ds(pl.multiple_of(s * 4, 4), 4), :]

        return 0

    lax.fori_loop(0, asked_ref.shape[0], add, 0)
    radii = radius_ref[...]
    scale = time_step / (radii * radii * radii)
    alive = state_ref[:, 3, :]
    weight = force[:, 3, :]
    for c in range(3):
        contact = state_ref[:, c, :] * weight - alive * force[:, c, :]
        out_ref[c] = speed_ref[c] + scale * (contact + fluid_ref[c])


def on_device(
    positions,
    velocities,
    radius,
    sphere_cell,
    pair_route,
    pair_mine,
    pair_theirs,
    brick_owner,
    fluid_velocity,
    pressure_grad,
):
    f32 = jnp.float32
    sphere_total = positions.shape[2]
    blocks = sphere_total // WIDTH
    gy_count = lax.axis_size("gy")
    gx_count = lax.axis_size("gx")
    cells_dev = fluid_velocity.shape[2]
    rows = cells_dev // WIDTH
    pair_total = pair_route.shape[1]
    capacity = max(2, 2 * pair_total // gx_count)
    slot_total = gx_count * capacity
    params = pltpu.CompilerParams(vmem_limit_bytes=LIMIT)

    counts = {"gx": gx_count, "gy": gy_count}

    target = (lax.axis_index("gx") + 1 + pair_route[0, :, 0]) % gx_count
    pair_ids = jnp.arange(pair_total, dtype=jnp.int32)
    earlier = (target[:, None] == target[None, :]) & (pair_ids[None, :] < pair_ids[:, None])
    slot = target * capacity + jnp.sum(earlier.astype(jnp.int32), axis=1)
    match = slot[None, :] == jnp.arange(slot_total, dtype=jnp.int32)[:, None]
    wanted = jnp.sum(jnp.where(match, pair_theirs[0][None, :] + 1, 0), axis=1) - 1
    wanted = jnp.pad(
        wanted.reshape(gx_count, 1, capacity),
        ((0, 0), (0, 0), (0, WIDTH - capacity)),
        constant_values=-1,
    )
    fields = jnp.concatenate([fluid_velocity[:, 0], pressure_grad[:, 0]], axis=0)
    asked, table = exchange(counts, wanted, fields.reshape(6, rows, WIDTH))
    asked = asked[:, 0, :capacity].reshape(-1)

    states, served = pl.pallas_call(
        state_kernel,
        out_shape=(
            jax.ShapeDtypeStruct((blocks, 8, WIDTH), f32),
            jax.ShapeDtypeStruct((slot_total, 8, WIDTH), f32),
        ),
        in_specs=[SMEM] + [VMEM] * 4,
        out_specs=(VMEM, VMEM),
        compiler_params=params,
        name="states",
    )(
        asked,
        positions.reshape(3, blocks, WIDTH),
        velocities.reshape(3, blocks, WIDTH),
        radius.reshape(blocks, WIDTH),
        sphere_cell.reshape(blocks, WIDTH),
    )
    tile = math.gcd(sphere_total, 1024)
    fluid, deposit, partner = pl.pallas_call(
        functools.partial(fluid_kernel, tile, gx_count),
        out_shape=(
            jax.ShapeDtypeStruct((3, 1, sphere_total), f32),
            jax.ShapeDtypeStruct((gy_count, 3, rows, WIDTH), f32),
            jax.ShapeDtypeStruct((gx_count, capacity * 8, WIDTH), f32),
        ),
        in_specs=[SMEM] + [VMEM] * 5,
        out_specs=(VMEM, VMEM, VMEM),
        scratch_shapes=[
            pltpu.VMEM((gy_count * 6 * rows, 2 * WIDTH), jnp.bfloat16),
            pltpu.VMEM((gy_count * 3 * rows, WIDTH), f32),
            pltpu.SemaphoreType.DMA((gx_count,)),
            pltpu.SemaphoreType.DMA((gx_count,)),
        ],
        compiler_params=pltpu.CompilerParams(
            vmem_limit_bytes=LIMIT, collective_id=1, has_side_effects=True
        ),
        cost_estimate=pl.CostEstimate(flops=4000000000, bytes_accessed=1000000, transcendentals=0),
        name="fluid",
    )(
        brick_owner,
        sphere_cell,
        velocities,
        radius,
        table,
        served.reshape(gx_count, capacity * 8, WIDTH),
    )
    partner = partner.reshape(slot_total, 8, WIDTH)
    listed, back = pl.pallas_call(
        listed_kernel,
        out_shape=(
            jax.ShapeDtypeStruct((blocks, 8, WIDTH), f32),
            jax.ShapeDtypeStruct((slot_total * 4, WIDTH), f32),
        ),
        in_specs=[SMEM, SMEM, VMEM, VMEM],
        out_specs=(VMEM, VMEM),
        compiler_params=params,
        name="listed",
    )(pair_mine[0], slot, states, partner)
    acc, returned, deposits = pl.pallas_call(
        functools.partial(local_kernel, counts),
        out_shape=(
            jax.ShapeDtypeStruct((blocks, 8, WIDTH), f32),
            jax.ShapeDtypeStruct((gx_count, capacity * 4, WIDTH), f32),
            jax.ShapeDtypeStruct(deposit.shape, f32),
        ),
        in_specs=[VMEM] * 4,
        out_specs=(VMEM, VMEM, VMEM),
        scratch_shapes=[pltpu.VMEM((8, WIDTH), f32)]
        + [pltpu.SemaphoreType.DMA((counts[axis],)) for axis in ("gx", "gx", "gy", "gy")],
        compiler_params=pltpu.CompilerParams(
            vmem_limit_bytes=LIMIT, collective_id=2, has_side_effects=True
        ),
        name="local",
    )(states, listed, back.reshape(gx_count, capacity * 4, WIDTH), deposit)
    returned = returned.reshape(slot_total * 4, WIDTH)
    speed = velocities.reshape(3, blocks, WIDTH)
    new_velocity, drag_source = pl.pallas_call(
        final_kernel,
        out_shape=(
            jax.ShapeDtypeStruct((3, blocks, WIDTH), f32),
            jax.ShapeDtypeStruct((3, rows, WIDTH), f32),
        ),
        in_specs=[SMEM] + [VMEM] * 7,
        out_specs=(VMEM, VMEM),
        scratch_shapes=[pltpu.VMEM((blocks, 8, WIDTH), f32)],
        compiler_params=params,
        name="final",
    )(
        asked,
        acc,
        returned,
        states,
        fluid.reshape(3, blocks, WIDTH),
        speed,
        radius.reshape(blocks, WIDTH),
        deposits,
    )
    return (new_velocity.reshape(3, 1, sphere_total), drag_source.reshape(3, 1, cells_dev))


def solution(mesh):
    placed = (
        P(None, "gx", "gy"),
        P(None, "gx", "gy"),
        P("gx", "gy"),
        P("gx", "gy"),
        P("gx", "gy", None),
        P("gx", "gy"),
        P("gx", "gy"),
        P("gx", None),
        P(None, "gx", "gy"),
        P(None, "gx", "gy"),
    )
    return jax.shard_map(
        on_device,
        mesh=mesh,
        in_specs=placed,
        out_specs=(P(None, "gx", "gy"), P(None, "gx", "gy")),
        check_vma=False,
    )
```
